32 devices in a mesh: groups: 2 (over y), gr: 4 (over z), gc: 4 (over x, core).
Axes of the slice: x: 2, y: 2, z: 4, core: 2. Of those that a mesh axis runs over, the one named last changes fastest.
Arguments:
- embeddings: bfloat16 [3072, 256], P(('groups', 'gr', 'gc')), parts along dimension 0, may hold values from -6 to 6
- thresholds: bfloat16 [3072], P(('groups', 'gr', 'gc')), parts along dimension 0, may hold values from 0.119628906 to 0.359375
- valid: int32 [3072], P(('groups', 'gr', 'gc')), parts along dimension 0, may hold values 0 or 1
Outputs:
- row_mix: bfloat16 [3072, 256], P(('groups', 'gr', 'gc')), parts along dimension 0
- partner_mix: bfloat16 [3072, 256], P(('groups', 'gr', 'gc')), parts along dimension 0
The draws below stay inside these ranges and needn't reach their ends.
There are 2 independent parts, one for each index of `groups`. The reference program is written for one: setup_inputs(seed, part) draws one part's arguments, and reference() takes and returns one part's arrays. A program takes and returns all parts, laid end to end along the dimension named above; each array names one. Nothing has to cross between parts.
All inputs are finite; a program needn't handle non-finite values. No bound on the sum of `valid` on one device may be relied on, other than what follows from the above.
Results may differ from the reference program's by a relative error of at most 0.0064.
Values may be sent and summed in bfloat16 or wider, within the bound.
A program may use at most 64 MiB of HBM per device.

```python
import math
import jax
import jax.numpy as jnp
from jax import lax

D = 256
ROWS = 1536


def plant(drawn, rng, least, largest):
    dims = drawn.shape
    spot = [jax.random.randint(jax.random.fold_in(rng, axis), (), 0, dims[axis]) for axis in range(len(dims))]
    drawn = drawn.at[tuple(spot)].set(least)
    longest = dims.index(max(dims))
    spot[longest] = (spot[longest] + 1) % dims[longest]
    return drawn.at[tuple(spot)].set(largest)


def block_levels(own_key, shape, shards, least, top_value):
    def one(axis_at, parts):
        draws = jax.random.uniform(jax.random.fold_in(jax.random.fold_in(own_key, 6), axis_at), (parts,), jnp.float32, least / len(shards), top_value / len(shards))
        return jnp.repeat(jnp.exp(draws), shape[axis_at] // parts).reshape((-1,) + (1,) * (len(shape) - axis_at - 1))

    loudness = one(*shards[0])
    for cut in shards[1:]:
        loudness = loudness * one(*cut)
    return loudness


def normal_values(stream_key, extent, deviation, reach, cuts=(), kind=jnp.bfloat16):
    result = deviation * jax.random.normal(stream_key, extent, jnp.float32)
    if cuts:
        result = result * block_levels(stream_key, extent, cuts, -0.22, 0.18)
    return jnp.clip(result, -reach, reach).astype(kind)


def setup_inputs(seed: int = 0, part: int = 0) -> dict:
    streams_of = jax.random.split(jax.random.key(seed), 4)
    own_keys = jax.random.split(jax.random.fold_in(streams_of[3], part), 4)
    return {
        "embeddings": normal_values(own_keys[0], (ROWS, D), 1.0, 6.0, ((0, 16),)),
        "thresholds": jnp.clip(jnp.exp(math.log(0.359375) - 1.0999719 * jax.random.uniform(own_keys[1], (ROWS,), jnp.float32) ** block_levels(own_keys[1], (ROWS,), ((0, 16),), -0.2, 0.2)), 0.119628906, 0.359375).astype(jnp.bfloat16),
        "valid": plant((jax.random.randint(own_keys[2], (ROWS,), 0, 8) < 7).astype(jnp.int32), jax.random.fold_in(own_keys[2], 1), 0, 1),
    }


sharpness = 40.0

def reference(embeddings, thresholds, valid):
    emb = embeddings.astype(jnp.float32)
    unit = (emb * lax.rsqrt(lax.optimization_barrier(jnp.sum(emb * emb, axis=1, keepdims=True)) + 1e-06)).astype(jnp.bfloat16)
    member = valid.astype(jnp.float32)
    limit = thresholds.astype(jnp.float32)
    width = min(512, ROWS)
    count = ROWS // width
    unit_blocks = unit.reshape(count, width, D)
    limit_blocks = limit.reshape(count, width)
    member_blocks = member.reshape(count, width)

    def step(carry, block):
        partner_sum, partner_total = carry
        rows_unit, rows_limit, rows_member = block
        scores = jnp.dot(rows_unit, unit.T, preferred_element_type=jnp.float32)
        weight = jax.nn.sigmoid(sharpness * (scores - rows_limit[:, None])) * rows_member[:, None] * member[None, :]
        weight_low = weight.astype(jnp.bfloat16)
        row_sum = jnp.dot(weight_low, unit, preferred_element_type=jnp.float32)
        row_total = lax.optimization_barrier(jnp.sum(weight, axis=1))
        partner_sum = partner_sum + jnp.dot(weight_low.T, rows_unit, preferred_element_type=jnp.float32)
        partner_total = partner_total + lax.optimization_barrier(jnp.sum(weight, axis=0))
        mixed = D ** 0.5 * row_sum / (1.0 + row_total[:, None])
        return ((partner_sum, partner_total), mixed.astype(jnp.bfloat16))
    start = (jnp.zeros((ROWS, D), jnp.float32), jnp.zeros((ROWS,), jnp.float32))
    (partner_sum, partner_total), row_mix = lax.scan(step, start, (unit_blocks, limit_blocks, member_blocks))
    partner_mix = (D ** 0.5 * partner_sum / (1.0 + partner_total[:, None])).astype(jnp.bfloat16)
    return (row_mix.reshape(ROWS, D), partner_mix)
```

```python
import functools

import jax
import jax.numpy as jnp
from jax import lax
from jax.experimental import pallas as pl
from jax.experimental.pallas import tpu as pltpu
from jax.sharding import PartitionSpec as P

sharpness = 40.0
LANES = 128
EXTRA = 16
FAR = 1e9
MESH = pl.DeviceIdType.MESH


def kernel(n_r, n_c, emb_ref, lim_ref, val_ref, row_ref, part_ref, buf, send_z, send_x, send_c, recv):
    rows, width = emb_ref.shape
    cols = width // LANES
    n_x = n_c // 2
    z = lax.axis_index("gr")
    g = lax.axis_index("gc")
    core = lax.rem(g, 2)
    xx = g // 2
    twin = g + 1 - 2 * core
    loop = functools.partial(lax.fori_loop, unroll=n_r <= 4)

    def z_peer(k):
        return lax.rem(z + k, n_r)

    def x_peer(k):
        return lax.rem(xx + k, n_x) * 2 + core

    def to(z_to, g_to):
        return {"gr": z_to, "gc": g_to}

    barrier = pltpu.get_barrier_semaphore()

    def greet(z_to, g_to):
        pl.semaphore_signal(barrier, inc=1, device_id=to(z_to, g_to), device_id_type=MESH)

    def each(first, last, do):
        def body(k, carry):
            do(k)
            return carry

        loop(first, last, body, 0)

    each(1, n_r, lambda k: greet(z_peer(k), g))
    each(1, n_x, lambda k: greet(z, x_peer(k)))
    greet(z, twin)

    emb = emb_ref[...].astype(jnp.float32)
    unit = (emb * lax.rsqrt(jnp.sum(emb * emb, axis=1, keepdims=True) + 1e-06)).astype(jnp.bfloat16)
    for c in range(cols):
        buf[z, g, c * rows:(c + 1) * rows, :] = unit[:, c * LANES:(c + 1) * LANES]
    lim_row = lim_ref[...].astype(jnp.float32).reshape(1, rows)
    val_row = val_ref[...].reshape(1, rows)
    far_row = jnp.where(val_row > 0, lim_row, FAR)
    far_pad = jnp.concatenate([far_row, jnp.full((1, LANES - rows), FAR, jnp.float32)], axis=1)
    buf[z, g, cols * rows:, :] = jnp.broadcast_to(far_pad, (EXTRA, LANES)).astype(jnp.bfloat16)

    pl.semaphore_wait(barrier, n_r + n_x - 1)

    def copy(z_of, g_of, sem, z_to, g_to):
        return pltpu.make_async_remote_copy(
            src_ref=buf.at[z_of, g_of],
            dst_ref=buf.at[z_of, g_of],
            send_sem=sem,
            recv_sem=recv.at[z_of, g_of],
            device_id=to(z_to, g_to),
            device_id_type=MESH,
        )

    def copy_z(k):
        return copy(z, g, send_z.at[k - 1], z_peer(k), g)

    def copy_x(p, k):
        return copy(z_peer(p), g, send_x.at[p, k - 1], z, x_peer(k))

    def copy_c(p, k):
        return copy(z_peer(p), x_peer(k), send_c.at[p, k], z, twin)

    def arrived(z_of, g_of):
        copy(z_of, g_of, send_z.at[0], z, twin).wait_recv()

    each(1, n_r, lambda k: copy_z(k).start())
    each(1, n_x, lambda k: copy_x(0, k).start())
    copy_c(0, 0).start()

    eye = lax.broadcasted_iota(jnp.int32, (rows, rows), 0) == lax.broadcasted_iota(jnp.int32, (rows, rows), 1)
    lim_col = jnp.sum(jnp.where(eye, lim_row, 0.0), axis=1, keepdims=True)
    val_col = jnp.sum(jnp.where(eye, val_row.astype(jnp.float32), 0.0), axis=1, keepdims=True)

    def pass_on(p):
        arrived(z_peer(p), g)
        each(1, n_x, lambda k: copy_x(p, k).start())
        copy_c(p, 0).start()

    def hand_over(p):
        def one(k):
            arrived(z_peer(p), x_peer(k))
            copy_c(p, k).start()

        each(1, n_x, one)

    def collect(p):
        def one(k):
            arrived(z_peer(p), lax.rem(xx + k, n_x) * 2 + 1 - core)

        each(0, n_x, one)

    def add(p, carry):
        sums, row_total, part_total = carry
        at = z_peer(p)
        others = jnp.concatenate(
            [buf[at, :, c * rows:(c + 1) * rows, :].reshape(n_c * rows, LANES) for c in range(cols)], axis=1
        )
        scores = lax.dot_general(
            unit, others, (((1,), (1,)), ((), ())), preferred_element_type=jnp.float32
        )
        far = jnp.concatenate(
            [buf[at, j, cols * rows:, :].astype(jnp.float32)[:1, :rows] for j in range(n_c)], axis=1
        )
        gone = far > 0.5 * FAR
        by_row = jnp.where(gone, 0.0, 0.5 + 0.5 * jnp.tanh(0.5 * sharpness * (scores - lim_col)))
        by_part = 0.5 + 0.5 * jnp.tanh(0.5 * sharpness * (scores - far))
        low = jnp.concatenate([by_row.astype(jnp.bfloat16), by_part.astype(jnp.bfloat16)], axis=0)
        sums = sums + jnp.dot(low, others, preferred_element_type=jnp.float32)
        row_total = row_total + jnp.sum(by_row, axis=1, keepdims=True)
        part_total = part_total + jnp.sum(by_part, axis=1, keepdims=True)
        return sums, row_total, part_total

    carry = (
        jnp.zeros((2 * rows, width), jnp.float32),
        jnp.zeros((rows, 1), jnp.float32),
        jnp.zeros((rows, 1), jnp.float32),
    )
    hand_over(0)

    def step(p, carry):
        pass_on(p)
        collect(p - 1)
        carry = add(p - 1, carry)
        hand_over(p)
        return carry

    carry = loop(1, n_r, step, carry)
    collect(n_r - 1)
    sums, row_total, part_total = add(n_r - 1, carry)

    scale = width**0.5 * val_col
    row_ref[...] = (sums[:rows] * (scale / (1.0 + row_total))).astype(jnp.bfloat16)
    part_ref[...] = (sums[rows:] * (scale / (1.0 + part_total))).astype(jnp.bfloat16)

    each(1, n_r, lambda k: copy_z(k).wait_send())

    def sent(p):
        each(1, n_x, lambda k: copy_x(p, k).wait_send())
        each(0, n_x, lambda k: copy_c(p, k).wait_send())

    each(0, n_r, sent)


def per_device(n_r, n_c, embeddings, thresholds, valid):
    rows, width = embeddings.shape
    vmem = pl.BlockSpec(memory_space=pltpu.VMEM)
    out = jax.ShapeDtypeStruct((rows, width), jnp.bfloat16)
    shard = (width // LANES) * rows + EXTRA
    return pl.pallas_call(
        functools.partial(kernel, n_r, n_c),
        out_shape=(out, out),
        in_specs=[vmem] * 3,
        out_specs=(vmem, vmem),
        scratch_shapes=[
            pltpu.VMEM((n_r, n_c, shard, LANES), jnp.bfloat16),
            pltpu.SemaphoreType.DMA((n_r - 1,)),
            pltpu.SemaphoreType.DMA((n_r, n_c // 2 - 1)),
            pltpu.SemaphoreType.DMA((n_r, n_c // 2)),
            pltpu.SemaphoreType.DMA((n_r, n_c)),
        ],
        compiler_params=pltpu.CompilerParams(
            collective_id=0, has_side_effects=True, vmem_limit_bytes=48 * 1024 * 1024
        ),
    )(embeddings, thresholds.reshape(1, rows), valid.reshape(1, rows))


def solution(mesh):
    return jax.shard_map(
        functools.partial(per_device, mesh.shape["gr"], mesh.shape["gc"]),
        mesh=mesh,
        in_specs=(
            P(("groups", "gr", "gc"), None),
            P(("groups", "gr", "gc")),
            P(("groups", "gr", "gc")),
        ),
        out_specs=(P(("groups", "gr", "gc"), None), P(("groups", "gr", "gc"), None)),
        check_vma=False,
    )
```

```python
import functools

import jax
import jax.numpy as jnp
from jax import lax
from jax.experimental import pallas as pl
from jax.experimental.pallas import tpu as pltpu
from jax.sharding import PartitionSpec as P

sharpness = 40.0
LANES = 128
EXTRA = 16
FAR = 1e9
MESH = pl.DeviceIdType.MESH


def kernel(
    n_r, n_x, emb_hbm, lim_hbm, val_hbm, row_ref, part_ref,
    buf, emb_ref, lim_ref, val_ref, send, send_c, recv, load,
):
    rows, width = emb_ref.shape
    cols = width // LANES
    z = lax.axis_index("gr")
    g = lax.axis_index("gc")
    core = lax.rem(g, 2)
    x = g // 2
    few = n_r * n_x <= 8

    loads = [
        pltpu.make_async_copy(src, dst, load.at[i])
        for i, (src, dst) in enumerate(((emb_hbm, emb_ref), (lim_hbm, lim_ref), (val_hbm, val_ref)))
    ]
    for one in loads:
        one.start()

    def plane(p):
        return lax.rem(z + p, n_r)

    def column(k):
        return lax.rem(x + k, n_x)

    def device(z_to, x_to, core_to):
        return {"gr": z_to, "gc": x_to * 2 + core_to}

    def each(first, last, do):
        def body(i, carry):
            do(lax.rem(i, n_r), i // n_r)
            return carry

        if few:
            for i in range(first, last):
                do(i % n_r, i // n_r)
        else:
            lax.fori_loop(first, last, body, 0)

    barrier = pltpu.get_barrier_semaphore()

    def greet(z_to, x_to, core_to):
        pl.semaphore_signal(barrier, inc=1, device_id=device(z_to, x_to, core_to), device_id_type=MESH)

    each(1, n_r * n_x, lambda p, k: greet(plane(p), column(k), core))
    greet(z, x, 1 - core)

    for one in loads:
        one.wait()
    emb = emb_ref[...].astype(jnp.float32)
    unit = (emb * lax.rsqrt(jnp.sum(emb * emb, axis=1, keepdims=True) + 1e-06)).astype(jnp.bfloat16)
    for c in range(cols):
        buf[z, x, core, c * rows:(c + 1) * rows, :] = unit[:, c * LANES:(c + 1) * LANES]
    lim_row = lim_ref[...].astype(jnp.float32)
    val_row = val_ref[...]
    far_row = jnp.where(val_row > 0, lim_row, FAR)
    far_pad = jnp.concatenate([far_row, jnp.full((1, LANES - rows), FAR, jnp.float32)], axis=1)
    buf[z, x, core, cols * rows:, :] = jnp.broadcast_to(far_pad, (EXTRA, LANES)).astype(jnp.bfloat16)

    eye = lax.broadcasted_iota(jnp.int32, (rows, rows), 0) == lax.broadcasted_iota(jnp.int32, (rows, rows), 1)
    lim_col = jnp.sum(jnp.where(eye, lim_row, 0.0), axis=1, keepdims=True)
    val_col = jnp.sum(jnp.where(eye, val_row.astype(jnp.float32), 0.0), axis=1, keepdims=True)

    pl.semaphore_wait(barrier, n_r * n_x)

    def copy(z_of, x_of, core_of, sem, to):
        return pltpu.make_async_remote_copy(
            src_ref=buf.at[z_of, x_of, core_of],
            dst_ref=buf.at[z_of, x_of, core_of],
            send_sem=sem,
            recv_sem=recv.at[z_of, x_of, core_of],
            device_id=to,
            device_id_type=MESH,
        )

    def out(p, k):
        return copy(z, x, core, send.at[p, k], device(plane(p), column(k), core))

    def over(p, k):
        return copy(plane(p), column(k), core, send_c.at[p, k], device(z, x, 1 - core))

    def arrived(p, k, core_of):
        copy(plane(p), column(k), core_of, send_c.at[0, 0], device(z, x, 1 - core)).wait_recv()

    if few:
        order = [(p, k) for k in reversed(range(n_x)) for p in range(n_r) if p or k]
        for p, k in order:
            out(p, k).start()
    else:
        each(1, n_r * n_x, lambda p, k: out(p, k).start())
    over(0, 0).start()

    def pass_on(p, k):
        arrived(p, k, core)
        over(p, k).start()

    def add(planes, k, carry):
        sums, row_total, part_total = carry
        others = jnp.concatenate(
            [
                jnp.concatenate(
                    [buf[plane(p), column(k), :, c * rows:(c + 1) * rows, :].reshape(2 * rows, LANES) for p in planes],
                    axis=0,
                )
                for c in range(cols)
            ],
            axis=1,
        )
        scores = lax.dot_general(
            unit, others, (((1,), (1,)), ((), ())), preferred_element_type=jnp.float32
        )
        far = jnp.concatenate(
            [
                buf[plane(p), column(k), j, cols * rows:, :].astype(jnp.float32)[:1, :rows]
                for p in planes
                for j in range(2)
            ],
            axis=1,
        )
        gone = far > 0.5 * FAR
        by_row = jnp.where(gone, 0.0, 0.5 + 0.5 * jnp.tanh(0.5 * sharpness * (scores - lim_col)))
        by_part = 0.5 + 0.5 * jnp.tanh(0.5 * sharpness * (scores - far))
        low = jnp.concatenate([by_row.astype(jnp.bfloat16), by_part.astype(jnp.bfloat16)], axis=0)
        sums = sums + jnp.dot(low, others, preferred_element_type=jnp.float32)
        row_total = row_total + jnp.sum(by_row, axis=1, keepdims=True)
        part_total = part_total + jnp.sum(by_part, axis=1, keepdims=True)
        return sums, row_total, part_total

    carry = (
        jnp.zeros((2 * rows, width), jnp.float32),
        jnp.zeros((rows, 1), jnp.float32),
        jnp.zeros((rows, 1), jnp.float32),
    )
    if few:
        for p in range(1, n_r):
            pass_on(p, 0)
        for p in range(n_r):
            arrived(p, 0, 1 - core)
        carry = add(range(n_r), 0, carry)
        half = (n_r + 1) // 2
        for k in range(1, n_x):
            for p in range(n_r):
                pass_on(p, k)
            for planes in (range(half), range(half, n_r)):
                for p in planes:
                    arrived(p, k, 1 - core)
                carry = add(planes, k, carry)
    else:
        each(1, n_r * n_x, pass_on)
        each(0, n_r * n_x, lambda p, k: arrived(p, k, 1 - core))

        def step(i, carry):
            return add((lax.rem(i, n_r),), i // n_r, carry)

        carry = lax.fori_loop(0, n_r * n_x, step, carry)
    sums, row_total, part_total = carry

    scale = width**0.5 * val_col
    row_ref[...] = (sums[:rows] * (scale / (1.0 + row_total))).astype(jnp.bfloat16)
    part_ref[...] = (sums[rows:] * (scale / (1.0 + part_total))).astype(jnp.bfloat16)

    each(1, n_r * n_x, lambda p, k: out(p, k).wait_send())
    each(0, n_r * n_x, lambda p, k: over(p, k).wait_send())


def per_device(n_r, n_x, embeddings, thresholds, valid):
    rows, width = embeddings.shape
    hbm = pl.BlockSpec(memory_space=pltpu.HBM)
    vmem = pl.BlockSpec(memory_space=pltpu.VMEM)
    out = jax.ShapeDtypeStruct((rows, width), jnp.bfloat16)
    shard = (width // LANES) * rows + EXTRA
    return pl.pallas_call(
        functools.partial(kernel, n_r, n_x),
        out_shape=(out, out),
        in_specs=[hbm] * 3,
        out_specs=(vmem, vmem),
        scratch_shapes=[
            pltpu.VMEM((n_r, n_x, 2, shard, LANES), jnp.bfloat16),
            pltpu.VMEM((rows, width), embeddings.dtype),
            pltpu.VMEM((1, rows), thresholds.dtype),
            pltpu.VMEM((1, rows), valid.dtype),
            pltpu.SemaphoreType.DMA((n_r, n_x)),
            pltpu.SemaphoreType.DMA((n_r, n_x)),
            pltpu.SemaphoreType.DMA((n_r, n_x, 2)),
            pltpu.SemaphoreType.DMA((3,)),
        ],
        compiler_params=pltpu.CompilerParams(
            collective_id=0, has_side_effects=True, vmem_limit_bytes=48 * 1024 * 1024
        ),
    )(embeddings, thresholds.reshape(1, rows), valid.reshape(1, rows))


def solution(mesh):
    return jax.shard_map(
        functools.partial(per_device, mesh.shape["gr"], mesh.shape["gc"] // 2),
        mesh=mesh,
        in_specs=(
            P(("groups", "gr", "gc"), None),
            P(("groups", "gr", "gc")),
            P(("groups", "gr", "gc")),
        ),
        out_specs=(P(("groups", "gr", "gc"), None), P(("groups", "gr", "gc"), None)),
        check_vma=False,
    )
```

```python
import functools

import jax
import jax.numpy as jnp
from jax import lax
from jax.experimental import pallas as pl
from jax.experimental.pallas import tpu as pltpu
from jax.sharding import PartitionSpec as P

sharpness = 40.0
LANES = 128
EXTRA = 16
FAR = 1e9
MESH = pl.DeviceIdType.MESH


def kernel(
    n_r, n_x, emb_hbm, lim_hbm, val_hbm, mix_ref,
    buf, emb_ref, lim_ref, val_ref, send_z, send_x, send_c, recv, load,
):
    rows, width = emb_ref.shape
    cols = width // LANES
    z = lax.axis_index("gr")
    g = lax.axis_index("gc")
    core = lax.rem(g, 2)
    x = g // 2
    few = n_r * n_x <= 8

    loads = [
        pltpu.make_async_copy(src, dst, load.at[i])
        for i, (src, dst) in enumerate(((emb_hbm, emb_ref), (lim_hbm, lim_ref), (val_hbm, val_ref)))
    ]
    for one in loads:
        one.start()

    def plane(p):
        if not few or n_r & (n_r - 1):
            return lax.rem(z + p, n_r)
        at, bit = z, 1
        while bit < n_r:
            if p & bit:
                at = at + bit - 2 * bit * lax.rem(z // bit, 2)
            bit *= 2
        return at

    def column(k):
        return lax.rem(x + k, n_x)

    def device(z_to, x_to, core_to):
        return {"gr": z_to, "gc": x_to * 2 + core_to}

    def each(first, last, do):
        def body(i, carry):
            do(lax.rem(i, n_r), i // n_r)
            return carry

        if few:
            for i in range(first, last):
                do(i % n_r, i // n_r)
        else:
            lax.fori_loop(first, last, body, 0)

    def each_x(do):
        def body(k, carry):
            do(k)
            return carry

        if few:
            for k in range(1, n_x):
                do(k)
        else:
            lax.fori_loop(1, n_x, body, 0)

    barrier = pltpu.get_barrier_semaphore()

    def greet(z_to, x_to, core_to):
        pl.semaphore_signal(barrier, inc=1, device_id=device(z_to, x_to, core_to), device_id_type=MESH)

    each(1, n_r, lambda p, k: greet(plane(p), x, core))
    each_x(lambda k: greet(z, column(k), core))
    greet(z, x, 1 - core)

    for one in loads:
        one.wait()
    emb = emb_ref[...].astype(jnp.float32)
    unit = (emb * lax.rsqrt(jnp.sum(emb * emb, axis=1, keepdims=True) + 1e-06)).astype(jnp.bfloat16)
    for c in range(cols):
        buf[z, x, core, c * rows:(c + 1) * rows, :] = unit[:, c * LANES:(c + 1) * LANES]
    lim_row = lim_ref[...].astype(jnp.float32)
    val_row = val_ref[...]
    far_row = jnp.where(val_row > 0, lim_row, FAR)
    far_pad = jnp.concatenate([far_row, jnp.full((1, LANES - rows), FAR, jnp.float32)], axis=1)
    buf[z, x, core, cols * rows:, :] = jnp.broadcast_to(far_pad, (EXTRA, LANES)).astype(jnp.bfloat16)

    eye = lax.broadcasted_iota(jnp.int32, (rows, rows), 0) == lax.broadcasted_iota(jnp.int32, (rows, rows), 1)
    lim_col = jnp.sum(jnp.where(eye, lim_row, 0.0), axis=1, keepdims=True)
    val_col = jnp.sum(jnp.where(eye, val_row.astype(jnp.float32), 0.0), axis=1, keepdims=True)

    pl.semaphore_wait(barrier, n_r + n_x - 1)

    def copy(z_of, x_of, core_of, sem, to):
        return pltpu.make_async_remote_copy(
            src_ref=buf.at[z_of, x_of, core_of],
            dst_ref=buf.at[z_of, x_of, core_of],
            send_sem=sem,
            recv_sem=recv.at[z_of, x_of, core_of],
            device_id=to,
            device_id_type=MESH,
        )

    def out(p):
        return copy(z, x, core, send_z.at[p], device(plane(p), x, core))

    def along(p, k):
        return copy(plane(p), x, core, send_x.at[p, k], device(z, column(k), core))

    def over(p, k):
        return copy(plane(p), column(k), core, send_c.at[p, k], device(z, x, 1 - core))

    def arrived(p, k, core_of):
        copy(plane(p), column(k), core_of, send_c.at[0, 0], device(z, x, 1 - core)).wait_recv()

    if few:
        near = [1] if n_r > 1 else []
        for p in [*range(2, n_r), *near]:
            out(p).start()
    else:
        each(1, n_r, lambda p, k: out(p).start())
    each_x(lambda k: along(0, k).start())
    over(0, 0).start()

    def from_plane(p, k=0):
        arrived(p, 0, core)
        each_x(lambda to: along(p, to).start())
        over(p, 0).start()

    def from_column(p):
        def one(k):
            arrived(p, k, core)
            over(p, k).start()

        each_x(one)

    def add(pieces, carry):
        sums, row_total, part_total = carry
        others = jnp.concatenate(
            [
                jnp.concatenate(
                    [buf[plane(p), column(k), :, c * rows:(c + 1) * rows, :].reshape(2 * rows, LANES) for p, k in pieces],
                    axis=0,
                )
                for c in range(cols)
            ],
            axis=1,
        )
        scores = lax.dot_general(
            unit, others, (((1,), (1,)), ((), ())), preferred_element_type=jnp.float32
        )
        far = jnp.concatenate(
            [
                buf[plane(p), column(k), j, cols * rows:, :].astype(jnp.float32)[:1, :rows]
                for p, k in pieces
                for j in range(2)
            ],
            axis=1,
        )
        gone = far > 0.5 * FAR
        by_row = jnp.where(gone, 0.0, 0.5 + 0.5 * jnp.tanh(0.5 * sharpness * (scores - lim_col)))
        by_part = 0.5 + 0.5 * jnp.tanh(0.5 * sharpness * (scores - far))
        low = jnp.concatenate([by_row.astype(jnp.bfloat16), by_part.astype(jnp.bfloat16)], axis=0)
        sums = sums + jnp.dot(low, others, preferred_element_type=jnp.float32)
        row_total = row_total + jnp.sum(by_row, axis=1, keepdims=True)
        part_total = part_total + jnp.sum(by_part, axis=1, keepdims=True)
        return sums, row_total, part_total

    carry = (
        jnp.zeros((2 * rows, width), jnp.float32),
        jnp.zeros((rows, 1), jnp.float32),
        jnp.zeros((rows, 1), jnp.float32),
    )
    if few:
        last = n_r - 1
        own = [(p, 0) for p in range(n_r)]
        early = [(p, k) for k in range(1, n_x) for p in range(last)]
        late = [(last, k) for k in range(1, n_x)]

        def settle(pieces, carry):
            for p, k in pieces:
                arrived(p, k, 1 - core)
            return add(pieces, carry) if pieces else carry

        for p in range(1, n_r):
            from_plane(p)
            if p < last:
                from_column(p - 1)
        if n_r > 1:
            from_column(last - 1)
        carry = settle(own, carry)
        from_column(last)
        carry = settle(early, carry)
        carry = settle(late, carry)
    else:
        each(1, n_r, from_plane)
        each(0, n_r, lambda p, k: from_column(p))
        each(0, n_r * n_x, lambda p, k: arrived(p, k, 1 - core))

        def step(i, carry):
            return add(((lax.rem(i, n_r), i // n_r),), carry)

        carry = lax.fori_loop(0, n_r * n_x, step, carry)
    sums, row_total, part_total = carry

    scale = width**0.5 * val_col
    mix_ref[:rows, :] = (sums[:rows] * (scale / (1.0 + row_total))).astype(jnp.bfloat16)
    mix_ref[rows:, :] = (sums[rows:] * (scale / (1.0 + part_total))).astype(jnp.bfloat16)

    each(1, n_r, lambda p, k: out(p).wait_send())
    each(0, n_r, lambda p, k: each_x(lambda to: along(p, to).wait_send()))
    each(0, n_r * n_x, lambda p, k: over(p, k).wait_send())


def per_device(n_r, n_x, embeddings, thresholds, valid):
    rows, width = embeddings.shape
    hbm = pl.BlockSpec(memory_space=pltpu.HBM)
    shard = (width // LANES) * rows + EXTRA
    mix = pl.pallas_call(
        functools.partial(kernel, n_r, n_x),
        out_shape=jax.ShapeDtypeStruct((2 * rows, width), jnp.bfloat16),
        in_specs=[hbm] * 3,
        out_specs=pl.BlockSpec(memory_space=pltpu.VMEM),
        scratch_shapes=[
            pltpu.VMEM((n_r, n_x, 2, shard, LANES), jnp.bfloat16),
            pltpu.VMEM((rows, width), embeddings.dtype),
            pltpu.VMEM((1, rows), thresholds.dtype),
            pltpu.VMEM((1, rows), valid.dtype),
            pltpu.SemaphoreType.DMA((n_r,)),
            pltpu.SemaphoreType.DMA((n_r, n_x)),
            pltpu.SemaphoreType.DMA((n_r, n_x)),
            pltpu.SemaphoreType.DMA((n_r, n_x, 2)),
            pltpu.SemaphoreType.DMA((3,)),
        ],
        compiler_params=pltpu.CompilerParams(
            collective_id=0, has_side_effects=True, vmem_limit_bytes=60 * 1024 * 1024
        ),
    )(embeddings, thresholds.reshape(1, rows), valid.reshape(1, rows))
    return mix[:rows], mix[rows:]


def solution(mesh):
    return jax.shard_map(
        functools.partial(per_device, mesh.shape["gr"], mesh.shape["gc"] // 2),
        mesh=mesh,
        in_specs=(
            P(("groups", "gr", "gc"), None),
            P(("groups", "gr", "gc")),
            P(("groups", "gr", "gc")),
        ),
        out_specs=(P(("groups", "gr", "gc"), None), P(("groups", "gr", "gc"), None)),
        check_vma=False,
    )
```

```python
import functools

import jax
import jax.numpy as jnp
from jax import lax
from jax.experimental import pallas as pl
from jax.experimental.pallas import tpu as pltpu
from jax.sharding import PartitionSpec as P

sharpness = 40.0
LANES = 128
EXTRA = 16
FAR = 1e9
MESH = pl.DeviceIdType.MESH


def kernel(
    n_r, n_x, emb_hbm, lim_hbm, val_hbm, mix_ref,
    buf, emb_ref, lim_ref, val_ref, send_z, send_x, send_c, recv, load,
):
    rows, width = emb_ref.shape
    cols = width // LANES
    z = lax.axis_index("gr")
    g = lax.axis_index("gc")
    core = lax.rem(g, 2)
    x = g // 2
    few = n_x == 2 and n_r <= 4

    loads = [
        pltpu.make_async_copy(src, dst, load.at[i])
        for i, (src, dst) in enumerate(((emb_hbm, emb_ref), (lim_hbm, lim_ref), (val_hbm, val_ref)))
    ]
    for one in loads:
        one.start()

    def plane(p):
        if not few or n_r & (n_r - 1):
            return lax.rem(z + p, n_r)
        at, bit = z, 1
        while bit < n_r:
            if p & bit:
                at = at + bit - 2 * bit * lax.rem(z // bit, 2)
            bit *= 2
        return at

    def column(k):
        return lax.rem(x + k, n_x)

    def device(z_to, x_to, core_to):
        return {"gr": z_to, "gc": x_to * 2 + core_to}

    def each(first, last, do):
        def body(i, carry):
            do(lax.rem(i, n_r), i // n_r)
            return carry

        if few:
            for i in range(first, last):
                do(i % n_r, i // n_r)
        else:
            lax.fori_loop(first, last, body, 0)

    def each_x(do):
        def body(k, carry):
            do(k)
            return carry

        if few:
            for k in range(1, n_x):
                do(k)
        else:
            lax.fori_loop(1, n_x, body, 0)

    barrier = pltpu.get_barrier_semaphore()

    def greet(z_to, x_to, core_to):
        pl.semaphore_signal(barrier, inc=1, device_id=device(z_to, x_to, core_to), device_id_type=MESH)

    each(1, n_r, lambda p, k: greet(plane(p), x, core))
    if few:
        greet(plane(1), column(1), core)
    each_x(lambda k: greet(z, column(k), core))
    greet(z, x, 1 - core)

    for one in loads:
        one.wait()
    emb = emb_ref[...].astype(jnp.float32)
    unit = (emb * lax.rsqrt(jnp.sum(emb * emb, axis=1, keepdims=True) + 1e-06)).astype(jnp.bfloat16)
    for c in range(cols):
        buf[z, x, core, c * rows:(c + 1) * rows, :] = unit[:, c * LANES:(c + 1) * LANES]
    lim_row = lim_ref[...].astype(jnp.float32)
    val_row = val_ref[...]
    far_row = jnp.where(val_row > 0, lim_row, FAR)
    far_pad = jnp.concatenate([far_row, jnp.full((1, LANES - rows), FAR, jnp.float32)], axis=1)
    buf[z, x, core, cols * rows:, :] = jnp.broadcast_to(far_pad, (EXTRA, LANES)).astype(jnp.bfloat16)

    eye = lax.broadcasted_iota(jnp.int32, (rows, rows), 0) == lax.broadcasted_iota(jnp.int32, (rows, rows), 1)
    lim_col = jnp.sum(jnp.where(eye, lim_row, 0.0), axis=1, keepdims=True)
    val_col = jnp.sum(jnp.where(eye, val_row.astype(jnp.float32), 0.0), axis=1, keepdims=True)

    pl.semaphore_wait(barrier, n_r + n_x - (0 if few else 1))

    def copy(z_of, x_of, core_of, sem, to):
        return pltpu.make_async_remote_copy(
            src_ref=buf.at[z_of, x_of, core_of],
            dst_ref=buf.at[z_of, x_of, core_of],
            send_sem=sem,
            recv_sem=recv.at[z_of, x_of, core_of],
            device_id=to,
            device_id_type=MESH,
        )

    def out(p):
        return copy(z, x, core, send_z.at[p], device(plane(p), x, core))

    def along(p, k):
        return copy(plane(p), x, core, send_x.at[p, k], device(z, column(k), core))

    def over(p, k):
        return copy(plane(p), column(k), core, send_c.at[p, k], device(z, x, 1 - core))

    def diag():
        return copy(z, x, core, send_x.at[1, 1], device(plane(1), column(1), core))

    def arrived(p, k, core_of):
        copy(plane(p), column(k), core_of, send_c.at[0, 0], device(z, x, 1 - core)).wait_recv()

    if few:
        near = [1] if n_r > 1 else []
        for p in [*near, *range(2, n_r)]:
            out(p).start()
    else:
        each(1, n_r, lambda p, k: out(p).start())
    each_x(lambda k: along(0, k).start())
    if few:
        diag().start()
    over(0, 0).start()

    def from_plane(p, k=0):
        arrived(p, 0, core)
        if not few or p != 1:
            each_x(lambda to: along(p, to).start())
        over(p, 0).start()

    def from_column(p):
        def one(k):
            arrived(p, k, core)
            over(p, k).start()

        each_x(one)

    def add(pieces, carry):
        sums, row_total, part_total = carry
        others = jnp.concatenate(
            [
                jnp.concatenate(
                    [buf[plane(p), column(k), :, c * rows:(c + 1) * rows, :].reshape(2 * rows, LANES) for p, k in pieces],
                    axis=0,
                )
                for c in range(cols)
            ],
            axis=1,
        )
        scores = lax.dot_general(
            unit, others, (((1,), (1,)), ((), ())), preferred_element_type=jnp.float32
        )
        far = jnp.concatenate(
            [
                buf[plane(p), column(k), j, cols * rows:, :].astype(jnp.float32)[:1, :rows]
                for p, k in pieces
                for j in range(2)
            ],
            axis=1,
        )
        gone = far > 0.5 * FAR
        by_row = jnp.where(gone, 0.0, 0.5 + 0.5 * jnp.tanh(0.5 * sharpness * (scores - lim_col)))
        by_part = 0.5 + 0.5 * jnp.tanh(0.5 * sharpness * (scores - far))
        low = jnp.concatenate([by_row.astype(jnp.bfloat16), by_part.astype(jnp.bfloat16)], axis=0)
        sums = sums + jnp.dot(low, others, preferred_element_type=jnp.float32)
        row_total = row_total + jnp.sum(by_row, axis=1, keepdims=True)
        part_total = part_total + jnp.sum(by_part, axis=1, keepdims=True)
        return sums, row_total, part_total

    carry = (
        jnp.zeros((2 * rows, width), jnp.float32),
        jnp.zeros((rows, 1), jnp.float32),
        jnp.zeros((rows, 1), jnp.float32),
    )
    if few:
        last = n_r - 1
        own = [(p, 0) for p in range(n_r)]
        early = [(p, k) for k in range(1, n_x) for p in range(last)]
        late = [(last, k) for k in range(1, n_x)]

        def settle(pieces, carry):
            for p, k in pieces:
                arrived(p, k, 1 - core)
            return add(pieces, carry) if pieces else carry

        for p in range(1, n_r):
            from_plane(p)
            if p < last:
                from_column(p - 1)
        if n_r > 1:
            from_column(last - 1)
        carry = settle(own, carry)
        from_column(last)
        carry = settle(early, carry)
        carry = settle(late, carry)
    else:
        each(1, n_r, from_plane)
        each(0, n_r, lambda p, k: from_column(p))
        each(0, n_r * n_x, lambda p, k: arrived(p, k, 1 - core))

        def step(i, carry):
            return add(((lax.rem(i, n_r), i // n_r),), carry)

        carry = lax.fori_loop(0, n_r * n_x, step, carry)
    sums, row_total, part_total = carry

    scale = width**0.5 * val_col
    mix_ref[:rows, :] = (sums[:rows] * (scale / (1.0 + row_total))).astype(jnp.bfloat16)
    mix_ref[rows:, :] = (sums[rows:] * (scale / (1.0 + part_total))).astype(jnp.bfloat16)

    each(1, n_r, lambda p, k: out(p).wait_send())
    each(0, n_r, lambda p, k: each_x(lambda to: along(p, to).wait_send()))
    each(0, n_r * n_x, lambda p, k: over(p, k).wait_send())


def per_device(n_r, n_x, embeddings, thresholds, valid):
    rows, width = embeddings.shape
    hbm = pl.BlockSpec(memory_space=pltpu.HBM)
    shard = (width // LANES) * rows + EXTRA
    mix = pl.pallas_call(
        functools.partial(kernel, n_r, n_x),
        out_shape=pltpu.VMEM((2 * rows, width), jnp.bfloat16),
        in_specs=[hbm] * 3,
        out_specs=pl.BlockSpec(memory_space=pltpu.VMEM),
        scratch_shapes=[
            pltpu.VMEM((n_r, n_x, 2, shard, LANES), jnp.bfloat16),
            pltpu.VMEM((rows, width), embeddings.dtype),
            pltpu.VMEM((1, rows), thresholds.dtype),
            pltpu.VMEM((1, rows), valid.dtype),
            pltpu.SemaphoreType.DMA((n_r,)),
            pltpu.SemaphoreType.DMA((n_r, n_x)),
            pltpu.SemaphoreType.DMA((n_r, n_x)),
            pltpu.SemaphoreType.DMA((n_r, n_x, 2)),
            pltpu.SemaphoreType.DMA((3,)),
        ],
        compiler_params=pltpu.CompilerParams(
            collective_id=0, has_side_effects=True, vmem_limit_bytes=60 * 1024 * 1024
        ),
    )(embeddings, thresholds.reshape(1, rows), valid.reshape(1, rows))
    return mix[:rows], mix[rows:]


def solution(mesh):
    return jax.shard_map(
        functools.partial(per_device, mesh.shape["gr"], mesh.shape["gc"] // 2),
        mesh=mesh,
        in_specs=(
            P(("groups", "gr", "gc"), None),
            P(("groups", "gr", "gc")),
            P(("groups", "gr", "gc")),
        ),
        out_specs=(P(("groups", "gr", "gc"), None), P(("groups", "gr", "gc"), None)),
        check_vma=False,
    )
```

```python
import functools

import jax
import jax.numpy as jnp
from jax import lax
from jax.experimental import pallas as pl
from jax.experimental.pallas import tpu as pltpu
from jax.sharding import PartitionSpec as P

sharpness = 40.0
LANES = 128
EXTRA = 16
FAR = 1e9
MESH = pl.DeviceIdType.MESH


def kernel(
    n_r, n_x, emb_hbm, lim_hbm, val_hbm, mix_ref,
    buf, emb_ref, lim_ref, val_ref, send_z, send_x, send_c, recv, load,
):
    rows, width = emb_ref.shape
    cols = width // LANES
    z = lax.axis_index("gr")
    g = lax.axis_index("gc")
    core = lax.rem(g, 2)
    x = g // 2
    few = n_x == 2 and n_r <= 4

    loads = [
        pltpu.make_async_copy(src, dst, load.at[i])
        for i, (src, dst) in enumerate(((emb_hbm, emb_ref), (lim_hbm, lim_ref), (val_hbm, val_ref)))
    ]
    for one in loads:
        one.start()

    def plane(p):
        if not few or n_r & (n_r - 1):
            return lax.rem(z + p, n_r)
        at, bit = z, 1
        while bit < n_r:
            if p & bit:
                at = at + bit - 2 * bit * lax.rem(z // bit, 2)
            bit *= 2
        return at

    def column(k):
        return lax.rem(x + k, n_x)

    def device(z_to, x_to, core_to):
        return {"gr": z_to, "gc": x_to * 2 + core_to}

    def each(first, last, do):
        def body(i, carry):
            do(lax.rem(i, n_r), i // n_r)
            return carry

        if few:
            for i in range(first, last):
                do(i % n_r, i // n_r)
        else:
            lax.fori_loop(first, last, body, 0)

    def each_x(do):
        def body(k, carry):
            do(k)
            return carry

        if few:
            for k in range(1, n_x):
                do(k)
        else:
            lax.fori_loop(1, n_x, body, 0)

    barrier = pltpu.get_barrier_semaphore()

    def greet(z_to, x_to, core_to):
        pl.semaphore_signal(barrier, inc=1, device_id=device(z_to, x_to, core_to), device_id_type=MESH)

    each(1, n_r, lambda p, k: greet(plane(p), x, core))
    if few:
        greet(plane(1), column(1), core)
    each_x(lambda k: greet(z, column(k), core))
    greet(z, x, 1 - core)

    for one in loads:
        one.wait()
    emb = emb_ref[...].astype(jnp.float32)
    unit = (emb * lax.rsqrt(jnp.sum(emb * emb, axis=1, keepdims=True) + 1e-06)).astype(jnp.bfloat16)
    for c in range(cols):
        buf[z, x, core, c * rows:(c + 1) * rows, :] = unit[:, c * LANES:(c + 1) * LANES]
    lim_row = lim_ref[...].astype(jnp.float32)
    val_row = val_ref[...]
    far_row = jnp.where(val_row > 0, lim_row, FAR)
    far_pad = jnp.concatenate([far_row, jnp.full((1, LANES - rows), FAR, jnp.float32)], axis=1)
    buf[z, x, core, cols * rows:, :] = jnp.broadcast_to(far_pad, (EXTRA, LANES)).astype(jnp.bfloat16)

    pl.semaphore_wait(barrier, n_r + n_x - (0 if few else 1))

    def copy(z_of, x_of, core_of, sem, to):
        return pltpu.make_async_remote_copy(
            src_ref=buf.at[z_of, x_of, core_of],
            dst_ref=buf.at[z_of, x_of, core_of],
            send_sem=sem,
            recv_sem=recv.at[z_of, x_of, core_of],
            device_id=to,
            device_id_type=MESH,
        )

    def out(p):
        return copy(z, x, core, send_z.at[p], device(plane(p), x, core))

    def along(p, k):
        return copy(plane(p), x, core, send_x.at[p, k], device(z, column(k), core))

    def over(p, k):
        return copy(plane(p), column(k), core, send_c.at[p, k], device(z, x, 1 - core))

    def diag():
        return copy(z, x, core, send_x.at[1, 1], device(plane(1), column(1), core))

    def arrived(p, k, core_of):
        copy(plane(p), column(k), core_of, send_c.at[0, 0], device(z, x, 1 - core)).wait_recv()

    if few:
        near = [1] if n_r > 1 else []
        for p in [*near, *range(2, n_r)]:
            out(p).start()
    else:
        each(1, n_r, lambda p, k: out(p).start())
    if few:
        diag().start()
    each_x(lambda k: along(0, k).start())
    over(0, 0).start()

    eye = lax.broadcasted_iota(jnp.int32, (rows, rows), 0) == lax.broadcasted_iota(jnp.int32, (rows, rows), 1)
    lim_col = jnp.sum(jnp.where(eye, lim_row, 0.0), axis=1, keepdims=True)
    val_col = jnp.sum(jnp.where(eye, val_row.astype(jnp.float32), 0.0), axis=1, keepdims=True)

    def from_plane(p, k=0):
        arrived(p, 0, core)
        if not few or p != 1:
            each_x(lambda to: along(p, to).start())
        over(p, 0).start()

    def from_column(p):
        def one(k):
            arrived(p, k, core)
            over(p, k).start()

        each_x(one)

    def add(pieces, carry):
        sums, row_total, part_total = carry
        others = jnp.concatenate(
            [
                jnp.concatenate(
                    [buf[plane(p), column(k), :, c * rows:(c + 1) * rows, :].reshape(2 * rows, LANES) for p, k in pieces],
                    axis=0,
                )
                for c in range(cols)
            ],
            axis=1,
        )
        scores = lax.dot_general(
            unit, others, (((1,), (1,)), ((), ())), preferred_element_type=jnp.float32
        )
        far = jnp.concatenate(
            [
                buf[plane(p), column(k), j, cols * rows:, :].astype(jnp.float32)[:1, :rows]
                for p, k in pieces
                for j in range(2)
            ],
            axis=1,
        )
        gone = far > 0.5 * FAR
        by_row = jnp.where(gone, 0.0, 0.5 + 0.5 * jnp.tanh(0.5 * sharpness * (scores - lim_col)))
        by_part = 0.5 + 0.5 * jnp.tanh(0.5 * sharpness * (scores - far))
        low = jnp.concatenate([by_row.astype(jnp.bfloat16), by_part.astype(jnp.bfloat16)], axis=0)
        sums = sums + jnp.dot(low, others, preferred_element_type=jnp.float32)
        row_total = row_total + jnp.sum(by_row, axis=1, keepdims=True)
        part_total = part_total + jnp.sum(by_part, axis=1, keepdims=True)
        return sums, row_total, part_total

    carry = (
        jnp.zeros((2 * rows, width), jnp.float32),
        jnp.zeros((rows, 1), jnp.float32),
        jnp.zeros((rows, 1), jnp.float32),
    )
    if few:
        last = n_r - 1
        own = [(p, 0) for p in range(n_r)]
        early = [(p, k) for k in range(1, n_x) for p in range(last)]
        late = [(last, k) for k in range(1, n_x)]

        def settle(pieces, carry):
            for p, k in pieces:
                arrived(p, k, 1 - core)
            return add(pieces, carry) if pieces else carry

        for p in range(1, n_r):
            from_plane(p)
            if p < last:
                from_column(p - 1)
        if n_r > 1:
            from_column(last - 1)
        carry = settle(own, carry)
        from_column(last)
        carry = settle(early, carry)
        carry = settle(late, carry)
    else:
        each(1, n_r, from_plane)
        each(0, n_r, lambda p, k: from_column(p))
        each(0, n_r * n_x, lambda p, k: arrived(p, k, 1 - core))

        def step(i, carry):
            return add(((lax.rem(i, n_r), i // n_r),), carry)

        carry = lax.fori_loop(0, n_r * n_x, step, carry)
    sums, row_total, part_total = carry

    scale = width**0.5 * val_col
    mix_ref[:rows, :] = (sums[:rows] * (scale / (1.0 + row_total))).astype(jnp.bfloat16)
    mix_ref[rows:, :] = (sums[rows:] * (scale / (1.0 + part_total))).astype(jnp.bfloat16)

    each(1, n_r, lambda p, k: out(p).wait_send())
    each(0, n_r, lambda p, k: each_x(lambda to: along(p, to).wait_send()))
    each(0, n_r * n_x, lambda p, k: over(p, k).wait_send())


def per_device(n_r, n_x, embeddings, thresholds, valid):
    rows, width = embeddings.shape
    hbm = pl.BlockSpec(memory_space=pltpu.HBM)
    shard = (width // LANES) * rows + EXTRA
    mix = pl.pallas_call(
        functools.partial(kernel, n_r, n_x),
        out_shape=pltpu.VMEM((2 * rows, width), jnp.bfloat16),
        in_specs=[hbm] * 3,
        out_specs=pl.BlockSpec(memory_space=pltpu.VMEM),
        scratch_shapes=[
            pltpu.VMEM((n_r, n_x, 2, shard, LANES), jnp.bfloat16),
            pltpu.VMEM((rows, width), embeddings.dtype),
            pltpu.VMEM((1, rows), thresholds.dtype),
            pltpu.VMEM((1, rows), valid.dtype),
            pltpu.SemaphoreType.DMA((n_r,)),
            pltpu.SemaphoreType.DMA((n_r, n_x)),
            pltpu.SemaphoreType.DMA((n_r, n_x)),
            pltpu.SemaphoreType.DMA((n_r, n_x, 2)),
            pltpu.SemaphoreType.DMA((3,)),
        ],
        compiler_params=pltpu.CompilerParams(
            collective_id=0, has_side_effects=True, vmem_limit_bytes=60 * 1024 * 1024
        ),
    )(embeddings, thresholds.reshape(1, rows), valid.reshape(1, rows))
    return mix[:rows], mix[rows:]


def solution(mesh):
    return jax.shard_map(
        functools.partial(per_device, mesh.shape["gr"], mesh.shape["gc"] // 2),
        mesh=mesh,
        in_specs=(
            P(("groups", "gr", "gc"), None),
            P(("groups", "gr", "gc")),
            P(("groups", "gr", "gc")),
        ),
        out_specs=(P(("groups", "gr", "gc"), None), P(("groups", "gr", "gc"), None)),
        check_vma=False,
    )
```
